32 devices in a mesh: dp: 16 (over z, y, core), mp: 2 (over x).
Axes of the slice: x: 2, y: 2, z: 4, core: 2. Of those that a mesh axis runs over, the one named last changes fastest.
Arguments:
- queries: bfloat16 [8192, 1024], P('dp', 'mp'), may hold values from -20 to 20
- passages: bfloat16 [65536, 1024], P('dp', 'mp'), may hold values from -6 to 6
- positives: int32 [8192], P('dp'), may hold values from 0 to 4095, as said below
- negatives: int32 [16, 16], replicated, may hold values from -1 to 31, as said below
Outputs:
- losses: float32 [8192], P('dp')
- query_grad: float32 [8192, 1024], P('dp', 'mp')
- passage_grad: float32 [65536, 1024], P('dp', 'mp')
The draws below stay inside these ranges and needn't reach their ends.
Inputs may be any that keep to these rules, and one draw needn't show every extreme that they name: Within each dp index the 512 positives of its query block are distinct. `negatives`: each row names between 4 and 16 blocks (entries >= 0); some row names 16.
All inputs are finite; a program needn't handle non-finite values.
Results may differ from the reference program's by a relative error of at most 0.0075.
Values may be sent and summed in bfloat16 or wider, within the bound.
A program may use at most 128 MiB of HBM per device.

```python
import jax
import jax.numpy as jnp
from jax import lax

D = 1024
QB = 512
PBS = 128
BLK_DEV = 32
CAND = 2560
N_DP = 16


def positive_table(key):
    base = jax.random.fold_in(key, 11)
    keys = jax.random.split(base, N_DP)
    rows = jax.vmap(lambda single: jax.random.permutation(single, PBS * BLK_DEV)[:QB])(keys)
    return rows.astype(jnp.int32)


def embed_pair(key):
    base = jax.random.fold_in(key, 37)
    key_pass, key_query = jax.random.split(base, 2)
    passages = jnp.clip(jax.random.normal(key_pass, (N_DP * PBS * BLK_DEV, D), jnp.float32), -6.0, 6.0)
    queries = jnp.clip(jax.random.normal(key_query, (N_DP * QB, D), jnp.float32), -6.0, 6.0)
    return (queries, passages)


def draw_queries(key, part):
    return embed_pair(key)[0].astype(jnp.bfloat16)


def draw_passages(key, part):
    return embed_pair(key)[1].astype(jnp.bfloat16)


def draw_positives(key, part):
    return positive_table(key).reshape(N_DP * QB)


def draw_negatives(key, part):
    base = jax.random.fold_in(key, 23)
    key_len, key_full, key_order, key_pick = jax.random.split(base, 4)
    lengths = jax.random.randint(key_len, (N_DP,), N_DP // 4, N_DP + 1)
    full_row = jax.random.randint(key_full, (), 0, N_DP)
    lengths = jnp.where(jnp.arange(N_DP) == full_row, N_DP, lengths)
    orders = jax.vmap(lambda single: jax.random.permutation(single, N_DP))(jax.random.split(key_order, N_DP))
    ranks = jnp.argsort(orders, axis=1, stable=True)
    present = ranks < lengths[:, None]
    picks = jax.random.randint(key_pick, (N_DP, N_DP), 0, BLK_DEV)
    return jnp.where(present, picks, -1).astype(jnp.int32)


def setup_inputs(seed: int = 0) -> dict:
    key_list = jax.random.split(jax.random.key(seed), 5)
    queries = draw_queries(jax.random.fold_in(key_list[4], 71), 0)
    passages = draw_passages(jax.random.fold_in(key_list[4], 71), 0)
    positives = draw_positives(jax.random.fold_in(key_list[4], 71), 0)
    negatives = draw_negatives(jax.random.fold_in(key_list[4], 71), 0)
    return dict(queries=queries, passages=passages, positives=positives, negatives=negatives)


def reference(queries, passages, positives, negatives):
    pass_dev = PBS * BLK_DEV
    factor = D ** -0.5
    blocks = passages.reshape(N_DP * BLK_DEV, PBS, D)
    owners = jnp.arange(N_DP, dtype=jnp.int32)
    inside = jnp.arange(PBS, dtype=jnp.int32)

    def one_block(carry, index):
        query_rows = lax.dynamic_slice_in_dim(queries, index * QB, QB, 0).astype(jnp.float32)
        chosen = lax.dynamic_slice_in_dim(positives, index * QB, QB, 0)
        global_pos = (index * pass_dev + chosen).astype(jnp.int32)
        wanted = lax.dynamic_index_in_dim(negatives, index, 0, keepdims=False)
        block_ids = (owners * BLK_DEV + jnp.maximum(wanted, 0)).astype(jnp.int32)
        negative_rows = jnp.take(blocks, block_ids, axis=0).reshape(N_DP * PBS, D)
        cands = jnp.concatenate([jnp.take(passages, global_pos, axis=0), negative_rows], 0).astype(jnp.float32)
        slot_ok = jnp.repeat(wanted >= 0, PBS)
        valid = jnp.concatenate([jnp.ones((QB,), bool), slot_ok], 0)
        scores = factor * jnp.dot(cands, query_rows.T)
        masked = jnp.where(valid[:, None], scores, jnp.float32(-1e30))
        top = jnp.max(masked, axis=0)
        total = jnp.sum(jnp.where(valid[:, None], jnp.exp(masked - top), jnp.float32(0.0)), axis=0)
        lse = top + jnp.log(total)
        own = jnp.diagonal(scores[:QB])
        loss = lse - own
        prob = jnp.where(valid[:, None], jnp.exp(masked - lse), jnp.float32(0.0))
        target = (jnp.arange(CAND)[:, None] == jnp.arange(QB)[None, :]).astype(jnp.float32)
        grad_scores = (prob - target).astype(jnp.bfloat16).astype(jnp.float32)
        query_grad = factor * jnp.dot(grad_scores.T, cands)
        cand_grad = factor * jnp.dot(grad_scores, query_rows)
        carry = carry.at[global_pos].add(cand_grad[:QB])
        neg_rows = (block_ids[:, None] * PBS + inside[None, :]).reshape(-1).astype(jnp.int32)
        carry = carry.at[neg_rows].add(cand_grad[QB:])
        return carry, (loss, query_grad)

    start = jnp.zeros((N_DP * pass_dev, D), jnp.float32)
    passage_grad, (losses, query_grad) = lax.scan(one_block, start, jnp.arange(N_DP, dtype=jnp.int32))
    return losses.reshape(N_DP * QB), query_grad.reshape(N_DP * QB, D), passage_grad
```

```python
import functools

import jax
import jax.numpy as jnp
from jax import lax
from jax.experimental import pallas as pl
from jax.experimental.pallas import tpu as pltpu
from jax.sharding import PartitionSpec as P

PBS = 128
MESH = pl.DeviceIdType.MESH
F32 = jnp.float32
BF16 = jnp.bfloat16


def exchange_kernel(
    dp, mp, factor,
    neg, pos, q, passages,
    losses, query_grad, pos_grad, returned,
    table, sending, cands, others, q_other, scores, grads, back, stats, top_ref,
    load_sem, f_send, f_recv, x_send, x_recv, q_send, q_recv,
    s_send, s_recv, g_send, g_recv, r_send, r_recv,
):
    me = lax.axis_index("dp")
    mine = lax.axis_index("mp")
    rows, width = q.shape
    pos_blocks = rows // PBS
    neg_groups = dp // mp
    groups = (dp + pos_blocks) // mp
    half = neg_groups // 2

    def partner(s):
        out = me
        bit = 1
        while bit < dp:
            out = out + bit * ((s // bit) % 2) * (1 - 2 * ((me // bit) % 2))
            bit *= 2
        return out

    def peer(p):
        return lax.rem(mine + p, mp)

    def ordered(k):
        return (1 - k % 2) * half + k // 2

    def fetch(s):
        return pltpu.make_async_remote_copy(
            src_ref=sending.at[s], dst_ref=cands.at[s],
            send_sem=f_send.at[s], recv_sem=f_recv.at[s],
            device_id=(partner(s), mine), device_id_type=MESH)

    def give_back(s):
        return pltpu.make_async_remote_copy(
            src_ref=back.at[s], dst_ref=returned.at[s],
            send_sem=r_send.at[s], recv_sem=r_recv.at[s],
            device_id=(partner(s), mine), device_id_type=MESH)

    def relay(p, t):
        return pltpu.make_async_remote_copy(
            src_ref=cands.at[t * mp + peer(p)], dst_ref=others.at[p - 1, t],
            send_sem=x_send.at[p - 1, t], recv_sem=x_recv.at[p - 1, t],
            device_id=(me, peer(p)), device_id_type=MESH)

    def share_queries(p):
        return pltpu.make_async_remote_copy(
            src_ref=q, dst_ref=q_other.at[p - 1],
            send_sem=q_send.at[p - 1], recv_sem=q_recv.at[p - 1],
            device_id=(me, peer(p)), device_id_type=MESH)

    def share_stats(p):
        return pltpu.make_async_remote_copy(
            src_ref=stats.at[mine], dst_ref=stats.at[mine],
            send_sem=s_send.at[p - 1], recv_sem=s_recv.at[p - 1],
            device_id=(me, peer(p)), device_id_type=MESH)

    def share_grads(p, t):
        return pltpu.make_async_remote_copy(
            src_ref=grads.at[t * mp + mine], dst_ref=grads.at[t * mp + mine],
            send_sem=g_send.at[p - 1, t], recv_sem=g_recv.at[p - 1, t],
            device_id=(me, peer(p)), device_id_type=MESH)

    def stats_from(p):
        source = lax.rem(mine + mp - p, mp)
        return pltpu.make_async_remote_copy(
            src_ref=stats.at[source], dst_ref=stats.at[source],
            send_sem=s_send.at[p - 1], recv_sem=s_recv.at[p - 1],
            device_id=(me, peer(p)), device_id_type=MESH)

    def grads_from(p, t):
        source = lax.rem(mine + mp - p, mp)
        return pltpu.make_async_remote_copy(
            src_ref=grads.at[t * mp + source], dst_ref=grads.at[t * mp + source],
            send_sem=g_send.at[p - 1, t], recv_sem=g_recv.at[p - 1, t],
            device_id=(me, peer(p)), device_id_type=MESH)

    load = pltpu.make_async_copy(passages, table, load_sem)
    load.start()
    barrier = pltpu.get_barrier_semaphore()

    @pl.loop(1, dp)
    def _(s):
        pl.semaphore_signal(barrier, inc=1, device_id=(partner(s), mine), device_id_type=MESH)

    for p in range(1, mp):
        pl.semaphore_signal(barrier, inc=1, device_id=(me, peer(p)), device_id_type=MESH)
    load.wait()
    pl.semaphore_wait(barrier, dp - 1 + mp - 1)

    def block_for(s):
        return table[jnp.maximum(neg[partner(s), me], 0)]

    cands[0] = block_for(0)

    @pl.loop(0, neg_groups)
    def _(k):
        t = ordered(k)
        for c in range(mp):
            s = t * mp + c

            @pl.when(s > 0)
            def _():
                sending[s] = block_for(s)
                fetch(s).start()

    for p in range(1, mp):
        share_queries(p).start()

    query_grad[...] = jnp.zeros_like(query_grad)
    chunk = 4 * PBS

    @pl.loop(0, table.shape[0] // 4)
    def _(c):
        ids = lax.broadcasted_iota(jnp.int32, (rows, chunk), 1) + c * chunk
        pick = jnp.where(ids == pos[...], 1.0, 0.0).astype(BF16)
        part = table[pl.ds(c * 4, 4)].reshape(chunk, width)
        query_grad[...] += jnp.dot(pick, part, preferred_element_type=F32)

    for b in range(pos_blocks):
        cands[dp + b] = query_grad[b * PBS:(b + 1) * PBS, :].astype(BF16)
    for t in range(neg_groups, groups):
        for p in range(1, mp):
            relay(p, t).start()
    for p in range(1, mp):
        share_queries(p).wait_recv()

    top_ref[...] = jnp.full(top_ref.shape, -1e30, F32)

    def dot_nt(a, b):
        return lax.dot_general(a, b, (((1,), (1,)), ((), ())), preferred_element_type=F32)

    def score(t):
        total = dot_nt(cands[t * mp + mine], q[...])
        for p in range(1, mp):
            relay(p, t).wait_recv()
            total = total + dot_nt(others[p - 1, t], q_other[p - 1])
        return factor * total

    def note_top(value):
        top_ref[0:1, :] = jnp.maximum(top_ref[0:1, :], jnp.max(value, axis=0, keepdims=True))

    def score_negative(t):
        ok = neg[me, partner(t * mp + mine)] >= 0
        value = jnp.where(ok, score(t), F32(-1e30))
        scores[t] = value
        note_top(value)

    def is_target(t):
        row = lax.broadcasted_iota(jnp.int32, (PBS, rows), 0) + (t * mp + mine - dp) * PBS
        return row == lax.broadcasted_iota(jnp.int32, (PBS, rows), 1)

    own = jnp.zeros((1, rows), F32)
    for t in range(neg_groups, groups):
        value = score(t)
        scores[t] = value
        note_top(value)
        own = own + jnp.sum(jnp.where(is_target(t), value, F32(0.0)), axis=0, keepdims=True)
    stats[mine, 2:3, :] = own

    @pl.loop(0, neg_groups)
    def _(k):
        t = ordered(k)
        for c in range(mp):
            @pl.when(t * mp + c > 0)
            def _():
                fetch(t * mp + c).wait_recv()
        for p in range(1, mp):
            relay(p, t).start()

        @pl.when(k > 0)
        def _():
            score_negative(ordered(k - 1))

    score_negative(ordered(neg_groups - 1))

    top = top_ref[0:1, :]

    @pl.loop(0, groups, init_carry=jnp.zeros((1, rows), F32))
    def total(t, carry):
        return carry + jnp.sum(jnp.exp(scores[t] - top), axis=0, keepdims=True)

    stats[mine, 0:1, :] = top
    stats[mine, 1:2, :] = total
    for p in range(1, mp):
        share_stats(p).start()
    for p in range(1, mp):
        stats_from(p).wait_recv()
    whole_top = stats[0, 0:1, :]
    for i in range(1, mp):
        whole_top = jnp.maximum(whole_top, stats[i, 0:1, :])
    whole = jnp.zeros((1, rows), F32)
    own_score = jnp.zeros((1, rows), F32)
    for i in range(mp):
        whole = whole + stats[i, 1:2, :] * jnp.exp(stats[i, 0:1, :] - whole_top)
        own_score = own_score + stats[i, 2:3, :]
    lse = whole_top + jnp.log(whole)
    losses[...] = lse - own_score
    top_ref[1:2, :] = lse

    def candidate_grad(i):
        return factor * jnp.dot(grads[i], q[...], preferred_element_type=F32)

    def send_back(s):
        back[s] = candidate_grad(s).astype(BF16)

        @pl.when(s > 0)
        def _():
            give_back(s).start()

    @pl.loop(0, neg_groups)
    def _(k):
        t = ordered(k)
        grads[t * mp + mine] = jnp.exp(scores[t] - top_ref[1:2, :]).astype(BF16)
        for p in range(1, mp):
            share_grads(p, t).start()
        send_back(t * mp + mine)

    for t in range(neg_groups, groups):
        prob = jnp.exp(scores[t] - top_ref[1:2, :])
        grads[t * mp + mine] = (prob - jnp.where(is_target(t), F32(1.0), F32(0.0))).astype(BF16)
        for p in range(1, mp):
            share_grads(p, t).start()

    @pl.loop(0, neg_groups)
    def _(k):
        t = ordered(k)
        for p in range(1, mp):
            grads_from(p, t).wait_recv()
            send_back(t * mp + lax.rem(mine + mp - p, mp))

    keep = pltpu.make_async_copy(back.at[0], returned.at[0], load_sem)
    keep.start()
    for t in range(neg_groups, groups):
        for p in range(1, mp):
            grads_from(p, t).wait_recv()
    for b in range(pos_blocks):
        pos_grad[b * PBS:(b + 1) * PBS, :] = candidate_grad(dp + b)
    query_grad[...] = jnp.zeros_like(query_grad)

    @pl.loop(0, groups)
    def _(t):
        g = grads[pl.ds(t * mp, mp)].reshape(mp * PBS, rows)
        c = cands[pl.ds(t * mp, mp)].reshape(mp * PBS, width)
        query_grad[...] += factor * lax.dot_general(
            g, c, (((0,), (0,)), ((), ())), preferred_element_type=F32)

    keep.wait()

    @pl.loop(1, dp)
    def _(s):
        fetch(s).wait_send()
        give_back(s).wait()

    for p in range(1, mp):
        share_queries(p).wait_send()
        share_stats(p).wait_send()

        @pl.loop(0, groups)
        def _(t):
            relay(p, t).wait_send()
            share_grads(p, t).wait_send()


def assemble_kernel(dp, per, me_ref, neg, pos, pos_grad, returned, out, high, low):
    step = pl.program_id(0)
    me = me_ref[0]
    rows, width = pos_grad.shape
    span = per * PBS

    @pl.when(step == 0)
    def _():
        value = pos_grad[...]
        top = value.astype(BF16)
        high[...] = top
        low[...] = (value - top.astype(F32)).astype(BF16)

    ids = lax.broadcasted_iota(jnp.int32, (span, rows), 0) + step * span
    pick = jnp.where(ids == pos[...], 1.0, 0.0).astype(BF16)
    value = jnp.dot(pick, high[...], preferred_element_type=F32) + jnp.dot(
        pick, low[...], preferred_element_type=F32)
    out[...] = value.reshape(per, PBS, width)

    @pl.loop(0, dp)
    def _(s):
        block = neg[me ^ s, me] - step * per

        @pl.when((block >= 0) & (block < per))
        def _():
            out[block] += returned[s].astype(F32)


def body(queries, passages, positives, negatives):
    dp = lax.axis_size("dp")
    mp = lax.axis_size("mp")
    rows, width = queries.shape
    factor = (width * mp) ** (-0.5)
    block_count = passages.shape[0] // PBS
    blocks = passages.reshape(block_count, PBS, width)
    total_blocks = dp + rows // PBS
    groups = total_blocks // mp
    vmem = pl.BlockSpec(memory_space=pltpu.VMEM)
    smem = pl.BlockSpec(memory_space=pltpu.SMEM)
    anywhere = pl.BlockSpec(memory_space=pl.ANY)
    dma = pltpu.SemaphoreType.DMA
    losses, query_grad, pos_grad, returned = pl.pallas_call(
        functools.partial(exchange_kernel, dp, mp, factor),
        out_shape=(
            jax.ShapeDtypeStruct((1, rows), F32),
            jax.ShapeDtypeStruct((rows, width), F32),
            jax.ShapeDtypeStruct((rows, width), F32),
            jax.ShapeDtypeStruct((dp, PBS, width), BF16),
        ),
        in_specs=[smem, vmem, vmem, anywhere],
        out_specs=(vmem, vmem, vmem, anywhere),
        scratch_shapes=[
            pltpu.VMEM((block_count, PBS, width), BF16),
            pltpu.VMEM((dp, PBS, width), BF16),
            pltpu.VMEM((total_blocks, PBS, width), BF16),
            pltpu.VMEM((mp - 1, groups, PBS, width), BF16),
            pltpu.VMEM((mp - 1, rows, width), BF16),
            pltpu.VMEM((groups, PBS, rows), F32),
            pltpu.VMEM((total_blocks, PBS, rows), BF16),
            pltpu.VMEM((dp, PBS, width), BF16),
            pltpu.VMEM((mp, 8, rows), F32),
            pltpu.VMEM((8, rows), F32),
            dma, dma((dp,)), dma((dp,)), dma((mp - 1, groups)), dma((mp - 1, groups)),
            dma((mp - 1,)), dma((mp - 1,)), dma((mp - 1,)), dma((mp - 1,)),
            dma((mp - 1, groups)), dma((mp - 1, groups)), dma((dp,)), dma((dp,)),
        ],
        compiler_params=pltpu.CompilerParams(
            collective_id=0, has_side_effects=True, vmem_limit_bytes=50 * 2**20),
    )(negatives, positives.reshape(rows, 1), queries, blocks)
    per = 4
    whole = lambda *shape: pl.BlockSpec(shape, lambda k: (0,) * len(shape))
    passage_grad = pl.pallas_call(
        functools.partial(assemble_kernel, dp, per),
        grid=(block_count // per,),
        out_shape=jax.ShapeDtypeStruct((block_count, PBS, width), F32),
        in_specs=[smem, smem, whole(1, rows), whole(rows, width), whole(dp, PBS, width)],
        out_specs=pl.BlockSpec((per, PBS, width), lambda k: (k, 0, 0)),
        scratch_shapes=[pltpu.VMEM((rows, width), BF16), pltpu.VMEM((rows, width), BF16)],
        compiler_params=pltpu.CompilerParams(vmem_limit_bytes=40 * 2**20),
    )(lax.axis_index("dp").reshape(1).astype(jnp.int32), negatives,
      positives.reshape(1, rows), pos_grad, returned)
    return losses.reshape(rows), query_grad, passage_grad.reshape(block_count * PBS, width)


def solution(mesh):
    in_specs = (P("dp", "mp"), P("dp", "mp"), P("dp"), P())
    out_specs = (P("dp"), P("dp", "mp"), P("dp", "mp"))
    return jax.shard_map(body, mesh=mesh, in_specs=in_specs, out_specs=out_specs, check_vma=False)
```

```python
import functools
import math

import jax
import jax.numpy as jnp
from jax import lax
from jax.experimental import pallas as pl
from jax.experimental.pallas import tpu as pltpu
from jax.sharding import PartitionSpec as P

PBS = 128
MESH = pl.DeviceIdType.MESH
F32 = jnp.float32
BF16 = jnp.bfloat16


def exchange_kernel(
    dp, mp, factor,
    neg_hbm, pos_hbm, q_hbm, passages,
    losses, query_grad, base, returned,
    neg, pos, q, high, low, table, sending, cands, others, q_other, scores, grads, back, stats, top_ref,
    load_sem, neg_sem, pos_sem, q_sem, f_send, f_recv, x_send, x_recv, q_send, q_recv,
    s_send, s_recv, g_send, g_recv, r_send, r_recv,
):
    me = lax.axis_index("dp")
    mine = lax.axis_index("mp")
    rows, width = q.shape
    pos_blocks = rows // PBS
    neg_groups = dp // mp
    groups = (dp + pos_blocks) // mp
    half = neg_groups // 2

    def partner(s):
        out = me
        bit = 1
        while bit < dp:
            out = out + bit * ((s // bit) % 2) * (1 - 2 * ((me // bit) % 2))
            bit *= 2
        return out

    def peer(p):
        return lax.rem(mine + p, mp)

    def ordered(k):
        return (1 - k % 2) * half + k // 2

    def fetch(s):
        return pltpu.make_async_remote_copy(
            src_ref=sending.at[s], dst_ref=cands.at[s],
            send_sem=f_send.at[s], recv_sem=f_recv.at[s],
            device_id=(partner(s), mine), device_id_type=MESH)

    def give_back(s):
        return pltpu.make_async_remote_copy(
            src_ref=back.at[s], dst_ref=returned.at[s],
            send_sem=r_send.at[s], recv_sem=r_recv.at[s],
            device_id=(partner(s), mine), device_id_type=MESH)

    def relay(p, t):
        return pltpu.make_async_remote_copy(
            src_ref=cands.at[t * mp + peer(p)], dst_ref=others.at[p - 1, t],
            send_sem=x_send.at[p - 1, t], recv_sem=x_recv.at[p - 1, t],
            device_id=(me, peer(p)), device_id_type=MESH)

    def share_queries(p):
        return pltpu.make_async_remote_copy(
            src_ref=q, dst_ref=q_other.at[p - 1],
            send_sem=q_send.at[p - 1], recv_sem=q_recv.at[p - 1],
            device_id=(me, peer(p)), device_id_type=MESH)

    def share_stats(p):
        return pltpu.make_async_remote_copy(
            src_ref=stats.at[mine], dst_ref=stats.at[mine],
            send_sem=s_send.at[p - 1], recv_sem=s_recv.at[p - 1],
            device_id=(me, peer(p)), device_id_type=MESH)

    def share_grads(p, t):
        return pltpu.make_async_remote_copy(
            src_ref=grads.at[t * mp + mine], dst_ref=grads.at[t * mp + mine],
            send_sem=g_send.at[p - 1, t], recv_sem=g_recv.at[p - 1, t],
            device_id=(me, peer(p)), device_id_type=MESH)

    def stats_from(p):
        source = lax.rem(mine + mp - p, mp)
        return pltpu.make_async_remote_copy(
            src_ref=stats.at[source], dst_ref=stats.at[source],
            send_sem=s_send.at[p - 1], recv_sem=s_recv.at[p - 1],
            device_id=(me, peer(p)), device_id_type=MESH)

    def grads_from(p, t):
        source = lax.rem(mine + mp - p, mp)
        return pltpu.make_async_remote_copy(
            src_ref=grads.at[t * mp + source], dst_ref=grads.at[t * mp + source],
            send_sem=g_send.at[p - 1, t], recv_sem=g_recv.at[p - 1, t],
            device_id=(me, peer(p)), device_id_type=MESH)

    load = pltpu.make_async_copy(passages, table, load_sem)
    load.start()
    load_neg = pltpu.make_async_copy(neg_hbm, neg, neg_sem)
    load_neg.start()
    load_q = pltpu.make_async_copy(q_hbm, q, q_sem)
    load_q.start()
    load_pos = pltpu.make_async_copy(pos_hbm, pos, pos_sem)
    load_pos.start()
    barrier = pltpu.get_barrier_semaphore()

    @pl.loop(1, dp)
    def _(s):
        pl.semaphore_signal(barrier, inc=1, device_id=(partner(s), mine), device_id_type=MESH)

    for p in range(1, mp):
        pl.semaphore_signal(barrier, inc=1, device_id=(me, peer(p)), device_id_type=MESH)
    load_neg.wait()
    load_q.wait()
    load_pos.wait()
    load.wait()
    pl.semaphore_wait(barrier, dp - 1 + mp - 1)

    def block_for(s):
        return table[jnp.maximum(neg[partner(s), me], 0)]

    cands[0] = block_for(0)

    @pl.loop(0, neg_groups)
    def _(k):
        t = ordered(k)
        for c in range(mp):
            s = t * mp + c

            @pl.when(s > 0)
            def _():
                sending[s] = block_for(s)
                fetch(s).start()

    for p in range(1, mp):
        share_queries(p).start()

    query_grad[...] = jnp.zeros_like(query_grad)
    chunk = 4 * PBS

    column = jnp.transpose(jnp.broadcast_to(pos[...].astype(F32), (PBS, rows)))[:, 0:1]
    column = column.astype(jnp.int32)

    @pl.loop(0, table.shape[0] // 4)
    def _(c):
        ids = lax.broadcasted_iota(jnp.int32, (rows, chunk), 1) + c * chunk
        pick = jnp.where(ids == column, 1.0, 0.0).astype(BF16)
        part = table[pl.ds(c * 4, 4)].reshape(chunk, width)
        query_grad[...] += jnp.dot(pick, part, preferred_element_type=F32)

    for b in range(pos_blocks):
        cands[dp + b] = query_grad[b * PBS:(b + 1) * PBS, :].astype(BF16)
    for t in range(neg_groups, groups):
        for p in range(1, mp):
            relay(p, t).start()
    for p in range(1, mp):
        share_queries(p).wait_recv()

    top_ref[...] = jnp.full(top_ref.shape, -1e30, F32)

    def dot_nt(a, b):
        return lax.dot_general(a, b, (((1,), (1,)), ((), ())), preferred_element_type=F32)

    def score(t):
        total = dot_nt(cands[t * mp + mine], q[...])
        for p in range(1, mp):
            relay(p, t).wait_recv()
            total = total + dot_nt(others[p - 1, t], q_other[p - 1])
        return factor * total

    def note_top(value):
        top_ref[0:1, :] = jnp.maximum(top_ref[0:1, :], jnp.max(value, axis=0, keepdims=True))

    def score_negative(t):
        ok = neg[me, partner(t * mp + mine)] >= 0
        value = jnp.where(ok, score(t), F32(-1e30))
        scores[t] = value
        note_top(value)

    def is_target(t):
        row = lax.broadcasted_iota(jnp.int32, (PBS, rows), 0) + (t * mp + mine - dp) * PBS
        return row == lax.broadcasted_iota(jnp.int32, (PBS, rows), 1)

    own = jnp.zeros((1, rows), F32)
    for t in range(neg_groups, groups):
        value = score(t)
        scores[t] = value
        note_top(value)
        own = own + jnp.sum(jnp.where(is_target(t), value, F32(0.0)), axis=0, keepdims=True)
    stats[mine, 2:3, :] = own

    @pl.loop(0, neg_groups)
    def _(k):
        t = ordered(k)
        for c in range(mp):
            @pl.when(t * mp + c > 0)
            def _():
                fetch(t * mp + c).wait_recv()
        for p in range(1, mp):
            relay(p, t).start()

        @pl.when(k > 0)
        def _():
            score_negative(ordered(k - 1))

    score_negative(ordered(neg_groups - 1))

    top = top_ref[0:1, :]

    @pl.loop(0, groups, init_carry=jnp.zeros((1, rows), F32))
    def total(t, carry):
        return carry + jnp.sum(jnp.exp(scores[t] - top), axis=0, keepdims=True)

    stats[mine, 0:1, :] = top
    stats[mine, 1:2, :] = total
    for p in range(1, mp):
        share_stats(p).start()
    for p in range(1, mp):
        stats_from(p).wait_recv()
    whole_top = stats[0, 0:1, :]
    for i in range(1, mp):
        whole_top = jnp.maximum(whole_top, stats[i, 0:1, :])
    whole = jnp.zeros((1, rows), F32)
    own_score = jnp.zeros((1, rows), F32)
    for i in range(mp):
        whole = whole + stats[i, 1:2, :] * jnp.exp(stats[i, 0:1, :] - whole_top)
        own_score = own_score + stats[i, 2:3, :]
    lse = whole_top + jnp.log(whole)
    losses[...] = lse - own_score
    top_ref[1:2, :] = lse

    def candidate_grad(i):
        return factor * jnp.dot(grads[i], q[...], preferred_element_type=F32)

    def send_back(s):
        value = candidate_grad(s).astype(BF16)

        @pl.when(s > 0)
        def _():
            back[s] = value
            give_back(s).start()

        @pl.when(s == 0)
        def _():
            returned[0] = value

    @pl.loop(0, neg_groups)
    def _(k):
        t = ordered(k)
        grads[t * mp + mine] = jnp.exp(scores[t] - top_ref[1:2, :]).astype(BF16)
        for p in range(1, mp):
            share_grads(p, t).start()
        send_back(t * mp + mine)

    for t in range(neg_groups, groups):
        prob = jnp.exp(scores[t] - top_ref[1:2, :])
        grads[t * mp + mine] = (prob - jnp.where(is_target(t), F32(1.0), F32(0.0))).astype(BF16)
        for p in range(1, mp):
            share_grads(p, t).start()

    @pl.loop(0, neg_groups)
    def _(k):
        t = ordered(k)
        for p in range(1, mp):
            grads_from(p, t).wait_recv()
            send_back(t * mp + lax.rem(mine + mp - p, mp))

    for t in range(neg_groups, groups):
        for p in range(1, mp):
            grads_from(p, t).wait_recv()
    for b in range(pos_blocks):
        value = candidate_grad(dp + b)
        upper = value.astype(BF16)
        high[b * PBS:(b + 1) * PBS, :] = upper
        low[b * PBS:(b + 1) * PBS, :] = (value - upper.astype(F32)).astype(BF16)

    @pl.loop(0, table.shape[0] // 4)
    def _(c):
        ids = lax.broadcasted_iota(jnp.int32, (chunk, rows), 0) + c * chunk
        pick = jnp.where(ids == pos[...], 1.0, 0.0).astype(BF16)
        value = jnp.dot(pick, high[...], preferred_element_type=F32) + jnp.dot(
            pick, low[...], preferred_element_type=F32)
        base[pl.ds(c * 4, 4)] = value.reshape(4, PBS, width)

    query_grad[...] = jnp.zeros_like(query_grad)

    @pl.loop(0, groups)
    def _(t):
        g = grads[pl.ds(t * mp, mp)].reshape(mp * PBS, rows)
        c = cands[pl.ds(t * mp, mp)].reshape(mp * PBS, width)
        query_grad[...] += factor * lax.dot_general(
            g, c, (((0,), (0,)), ((), ())), preferred_element_type=F32)

    @pl.loop(1, dp)
    def _(s):
        fetch(s).wait_send()
        give_back(s).wait()

    for p in range(1, mp):
        share_queries(p).wait_send()
        share_stats(p).wait_send()

        @pl.loop(0, groups)
        def _(t):
            relay(p, t).wait_send()
            share_grads(p, t).wait_send()


def assemble_kernel(
    dp, me_ref, neg, losses_in, query_grad_in, base, returned,
    losses, query_grad, out, stage, state, sems, loss_sem, query_sem,
):
    me = me_ref[0]
    block_count = base.shape[0]
    keep_losses = pltpu.make_async_copy(losses_in, losses, loss_sem)
    keep_losses.start()
    keep_query = pltpu.make_async_copy(query_grad_in, query_grad, query_sem)
    keep_query.start()

    @pl.loop(0, block_count)
    def _(k):
        state[k] = 0

    @pl.loop(0, dp)
    def _(s):
        k = neg[me ^ s, me]

        @pl.when(k >= 0)
        def _():
            state[k] = 1

    def plain(k):
        return pltpu.make_async_copy(base.at[k], out.at[k], sems.at[k])

    @pl.loop(0, block_count)
    def _(k):
        @pl.when(state[k] == 0)
        def _():
            plain(k).start()

    @pl.loop(0, dp)
    def _(s):
        k = neg[me ^ s, me]

        @pl.when(k >= 0)
        def _():
            now = state[k]

            @pl.when(now == 1)
            def _():
                state[k] = 2 + s
                stage[s] = base[k] + returned[s].astype(F32)

            @pl.when(now > 1)
            def _():
                stage[now - 2] += returned[s].astype(F32)

    @pl.loop(0, dp)
    def _(s):
        k = neg[me ^ s, me]

        @pl.when(k >= 0)
        def _():
            @pl.when(state[k] == 2 + s)
            def _():
                pltpu.make_async_copy(stage.at[s], out.at[k], sems.at[k]).start()

    keep_losses.wait()
    keep_query.wait()

    @pl.loop(0, block_count)
    def _(k):
        plain(k).wait()


def body(queries, passages, positives, negatives):
    dp = lax.axis_size("dp")
    mp = lax.axis_size("mp")
    rows, width = queries.shape
    factor = (width * mp) ** (-0.5)
    block_count = passages.shape[0] // PBS
    blocks = passages.reshape(block_count, PBS, width)
    total_blocks = dp + rows // PBS
    groups = total_blocks // mp
    vmem = pl.BlockSpec(memory_space=pltpu.VMEM)
    smem = pl.BlockSpec(memory_space=pltpu.SMEM)
    hbm = pl.BlockSpec(memory_space=pltpu.HBM)
    dma = pltpu.SemaphoreType.DMA
    made = (
        jax.ShapeDtypeStruct((1, rows), F32),
        jax.ShapeDtypeStruct((rows, width), F32),
        jax.ShapeDtypeStruct((block_count, PBS, width), F32),
        jax.ShapeDtypeStruct((dp, PBS, width), BF16),
    )
    scratch = [
        pltpu.VMEM((1, rows), jnp.int32),
        pltpu.VMEM((rows, width), BF16),
        pltpu.VMEM((rows, width), BF16),
        pltpu.VMEM((rows, width), BF16),
        pltpu.VMEM((block_count, PBS, width), BF16),
        pltpu.VMEM((dp, PBS, width), BF16),
        pltpu.VMEM((total_blocks, PBS, width), BF16),
        pltpu.VMEM((mp - 1, groups, PBS, width), BF16),
        pltpu.VMEM((mp - 1, rows, width), BF16),
        pltpu.VMEM((groups, PBS, rows), F32),
        pltpu.VMEM((total_blocks, PBS, rows), BF16),
        pltpu.VMEM((dp, PBS, width), BF16),
        pltpu.VMEM((mp, 8, rows), F32),
        pltpu.VMEM((8, rows), F32),
    ]
    held = sum(math.prod(a.shape) * jnp.dtype(a.dtype).itemsize for a in (*made, *scratch))
    losses, query_grad, base, returned = pl.pallas_call(
        functools.partial(exchange_kernel, dp, mp, factor),
        out_shape=made,
        in_specs=[hbm, hbm, hbm, hbm],
        out_specs=(vmem, vmem, vmem, vmem),
        scratch_shapes=[
            pltpu.SMEM((dp, dp), jnp.int32),
            *scratch,
            dma, dma, dma, dma,
            dma((dp,)), dma((dp,)), dma((mp - 1, groups)), dma((mp - 1, groups)),
            dma((mp - 1,)), dma((mp - 1,)), dma((mp - 1,)), dma((mp - 1,)),
            dma((mp - 1, groups)), dma((mp - 1, groups)), dma((dp,)), dma((dp,)),
        ],
        compiler_params=pltpu.CompilerParams(
            collective_id=0, has_side_effects=True, vmem_limit_bytes=held + 4 * 2**20),
    )(*(pltpu.with_memory_space_constraint(a, pltpu.HBM) for a in (negatives, positives.reshape(1, rows), queries, blocks)))
    losses, query_grad, passage_grad = pl.pallas_call(
        functools.partial(assemble_kernel, dp),
        out_shape=made[:3],
        in_specs=[smem, smem, vmem, vmem, vmem, vmem],
        out_specs=(hbm, hbm, hbm),
        scratch_shapes=[
            pltpu.VMEM((dp, PBS, width), F32),
            pltpu.SMEM((block_count,), jnp.int32),
            dma((block_count,)), dma, dma,
        ],
        compiler_params=pltpu.CompilerParams(vmem_limit_bytes=24 * 2**20),
    )(lax.axis_index("dp").reshape(1).astype(jnp.int32), negatives,
      losses, query_grad, base, returned)
    return losses.reshape(rows), query_grad, passage_grad.reshape(block_count * PBS, width)


def solution(mesh):
    in_specs = (P("dp", "mp"), P("dp", "mp"), P("dp"), P())
    out_specs = (P("dp"), P("dp", "mp"), P("dp", "mp"))
    return jax.shard_map(body, mesh=mesh, in_specs=in_specs, out_specs=out_specs, check_vma=False)
```

```python
import functools
import math

import jax
import jax.numpy as jnp
from jax import lax
from jax.experimental import pallas as pl
from jax.experimental.pallas import tpu as pltpu
from jax.sharding import PartitionSpec as P

PBS = 128
WINDOW = 4
LAG = 2
FIRST = 2
MESH = pl.DeviceIdType.MESH
F32 = jnp.float32
BF16 = jnp.bfloat16


def exchange_kernel(
    dp, mp, factor,
    neg_hbm, pos_hbm, q_hbm, passages,
    losses, query_grad, base, returned,
    neg, pos, q, high, low, table, sending, cands, others, q_other, scores, grads, back, stats, top_ref,
    load_sem, neg_sem, pos_sem, q_sem, f_send, f_recv, x_send, x_recv, q_send, q_recv,
    s_send, s_recv, g_send, g_recv, r_send, r_recv,
):
    me = lax.axis_index("dp")
    mine = lax.axis_index("mp")
    rows, width = q.shape
    pos_blocks = rows // PBS
    neg_groups = dp // mp
    groups = (dp + pos_blocks) // mp
    half = neg_groups // 2

    def partner(s):
        out = me
        bit = 1
        while bit < dp:
            out = out + bit * ((s // bit) % 2) * (1 - 2 * ((me // bit) % 2))
            bit *= 2
        return out

    def peer(p):
        return lax.rem(mine + p, mp)

    def ordered(k):
        return (1 - k % 2) * half + k // 2

    def fetch(s):
        return pltpu.make_async_remote_copy(
            src_ref=sending.at[s], dst_ref=cands.at[s],
            send_sem=f_send.at[s], recv_sem=f_recv.at[s],
            device_id=(partner(s), mine), device_id_type=MESH)

    def give_back(s):
        return pltpu.make_async_remote_copy(
            src_ref=back.at[s], dst_ref=returned.at[s],
            send_sem=r_send.at[s], recv_sem=r_recv.at[s],
            device_id=(partner(s), mine), device_id_type=MESH)

    def relay(p, t):
        return pltpu.make_async_remote_copy(
            src_ref=cands.at[t * mp + peer(p)], dst_ref=others.at[p - 1, t],
            send_sem=x_send.at[p - 1, t], recv_sem=x_recv.at[p - 1, t],
            device_id=(me, peer(p)), device_id_type=MESH)

    def share_queries(p):
        return pltpu.make_async_remote_copy(
            src_ref=q, dst_ref=q_other.at[p - 1],
            send_sem=q_send.at[p - 1], recv_sem=q_recv.at[p - 1],
            device_id=(me, peer(p)), device_id_type=MESH)

    def share_stats(p):
        return pltpu.make_async_remote_copy(
            src_ref=stats.at[mine], dst_ref=stats.at[mine],
            send_sem=s_send.at[p - 1], recv_sem=s_recv.at[p - 1],
            device_id=(me, peer(p)), device_id_type=MESH)

    def share_grads(p, t):
        return pltpu.make_async_remote_copy(
            src_ref=grads.at[t * mp + mine], dst_ref=grads.at[t * mp + mine],
            send_sem=g_send.at[p - 1, t], recv_sem=g_recv.at[p - 1, t],
            device_id=(me, peer(p)), device_id_type=MESH)

    def stats_from(p):
        source = lax.rem(mine + mp - p, mp)
        return pltpu.make_async_remote_copy(
            src_ref=stats.at[source], dst_ref=stats.at[source],
            send_sem=s_send.at[p - 1], recv_sem=s_recv.at[p - 1],
            device_id=(me, peer(p)), device_id_type=MESH)

    def grads_from(p, t):
        source = lax.rem(mine + mp - p, mp)
        return pltpu.make_async_remote_copy(
            src_ref=grads.at[t * mp + source], dst_ref=grads.at[t * mp + source],
            send_sem=g_send.at[p - 1, t], recv_sem=g_recv.at[p - 1, t],
            device_id=(me, peer(p)), device_id_type=MESH)

    load = pltpu.make_async_copy(passages, table, load_sem)
    load.start()
    load_neg = pltpu.make_async_copy(neg_hbm, neg, neg_sem)
    load_neg.start()
    load_q = pltpu.make_async_copy(q_hbm, q, q_sem)
    load_q.start()
    load_pos = pltpu.make_async_copy(pos_hbm, pos, pos_sem)
    load_pos.start()
    barrier = pltpu.get_barrier_semaphore()

    @pl.loop(1, dp)
    def _(s):
        pl.semaphore_signal(barrier, inc=1, device_id=(partner(s), mine), device_id_type=MESH)

    for p in range(1, mp):
        pl.semaphore_signal(barrier, inc=1, device_id=(me, peer(p)), device_id_type=MESH)
    load_neg.wait()
    load_q.wait()
    load_pos.wait()
    load.wait()
    pl.semaphore_wait(barrier, dp - 1 + mp - 1)

    def block_for(s):
        return table[jnp.maximum(neg[partner(s), me], 0)]

    cands[0] = block_for(0)

    window = min(WINDOW, neg_groups)

    def send_group(k):
        for c in range(mp):
            s = ordered(k) * mp + c

            @pl.when(s > 0)
            def _():
                sending[s] = block_for(s)
                fetch(s).start()

    @pl.loop(0, window)
    def _(k):
        send_group(k)

    for p in range(1, mp):
        share_queries(p).start()

    query_grad[...] = jnp.zeros_like(query_grad)
    chunk = 4 * PBS

    column = jnp.transpose(jnp.broadcast_to(pos[...].astype(F32), (PBS, rows)))[:, 0:1]
    column = column.astype(jnp.int32)

    @pl.loop(0, table.shape[0] // 4)
    def _(c):
        ids = lax.broadcasted_iota(jnp.int32, (rows, chunk), 1) + c * chunk
        pick = jnp.where(ids == column, 1.0, 0.0).astype(BF16)
        part = table[pl.ds(c * 4, 4)].reshape(chunk, width)
        query_grad[...] += jnp.dot(pick, part, preferred_element_type=F32)

    for b in range(pos_blocks):
        cands[dp + b] = query_grad[b * PBS:(b + 1) * PBS, :].astype(BF16)
    for t in range(neg_groups, groups):
        for p in range(1, mp):
            relay(p, t).start()
    for p in range(1, mp):
        share_queries(p).wait_recv()

    top_ref[...] = jnp.full(top_ref.shape, -1e30, F32)
    top_ref[2:3, :] = jnp.zeros((1, rows), F32)

    def dot_nt(a, b):
        return lax.dot_general(a, b, (((1,), (1,)), ((), ())), preferred_element_type=F32)

    def score(t):
        total = dot_nt(cands[t * mp + mine], q[...])
        for p in range(1, mp):
            relay(p, t).wait_recv()
            total = total + dot_nt(others[p - 1, t], q_other[p - 1])
        return factor * total

    def note(value):
        before = top_ref[0:1, :]
        now = jnp.maximum(before, jnp.max(value, axis=0, keepdims=True))
        part = jnp.sum(jnp.exp(value - now), axis=0, keepdims=True)
        top_ref[2:3, :] = top_ref[2:3, :] * jnp.exp(before - now) + part
        top_ref[0:1, :] = now

    def score_negative(k):
        t = ordered(k)
        ok = neg[me, partner(t * mp + mine)] >= 0
        value = jnp.where(ok, score(t), F32(-1e30))
        scores[t] = value
        note(value)

    def is_target(t):
        row = lax.broadcasted_iota(jnp.int32, (PBS, rows), 0) + (t * mp + mine - dp) * PBS
        return row == lax.broadcasted_iota(jnp.int32, (PBS, rows), 1)

    def arrive(k):
        t = ordered(k)
        for c in range(mp):
            @pl.when(t * mp + c > 0)
            def _():
                fetch(t * mp + c).wait_recv()
        for p in range(1, mp):
            relay(p, t).start()

        @pl.when(k + window < neg_groups)
        def _():
            send_group(k + window)

    @pl.loop(0, half)
    def _(k):
        arrive(k)

    own = jnp.zeros((1, rows), F32)
    for t in range(neg_groups, groups):
        value = score(t)
        scores[t] = value
        note(value)
        own = own + jnp.sum(jnp.where(is_target(t), value, F32(0.0)), axis=0, keepdims=True)
    stats[mine, 2:3, :] = own

    @pl.loop(0, half - LAG)
    def _(k):
        score_negative(k)

    @pl.loop(half, neg_groups)
    def _(k):
        arrive(k)
        score_negative(k - LAG)

    @pl.loop(neg_groups - LAG, neg_groups)
    def _(k):
        score_negative(k)

    stats[mine, 0:1, :] = top_ref[0:1, :]
    stats[mine, 1:2, :] = top_ref[2:3, :]
    for p in range(1, mp):
        share_stats(p).start()
    for p in range(1, mp):
        stats_from(p).wait_recv()
    whole_top = stats[0, 0:1, :]
    for i in range(1, mp):
        whole_top = jnp.maximum(whole_top, stats[i, 0:1, :])
    whole = jnp.zeros((1, rows), F32)
    own_score = jnp.zeros((1, rows), F32)
    for i in range(mp):
        whole = whole + stats[i, 1:2, :] * jnp.exp(stats[i, 0:1, :] - whole_top)
        own_score = own_score + stats[i, 2:3, :]
    lse = whole_top + jnp.log(whole)
    losses[...] = lse - own_score
    top_ref[1:2, :] = lse

    def candidate_grad(i):
        return factor * jnp.dot(grads[i], q[...], preferred_element_type=F32)

    def send_back(s):
        value = candidate_grad(s).astype(BF16)

        @pl.when(s > 0)
        def _():
            back[s] = value
            give_back(s).start()

        @pl.when(s == 0)
        def _():
            returned[0] = value

    def share_negative(k):
        t = ordered(k)
        grads[t * mp + mine] = jnp.exp(scores[t] - top_ref[1:2, :]).astype(BF16)
        for p in range(1, mp):
            share_grads(p, t).start()
        send_back(t * mp + mine)

    def add_query_grad(t):
        g = grads[pl.ds(t * mp, mp)].reshape(mp * PBS, rows)
        c = cands[pl.ds(t * mp, mp)].reshape(mp * PBS, width)
        query_grad[...] += factor * lax.dot_general(
            g, c, (((0,), (0,)), ((), ())), preferred_element_type=F32)

    def finish_negative(k):
        t = ordered(k)
        for p in range(1, mp):
            grads_from(p, t).wait_recv()
            send_back(t * mp + lax.rem(mine + mp - p, mp))
        add_query_grad(t)

    @pl.loop(0, FIRST)
    def _(k):
        share_negative(k)

    for t in range(neg_groups, groups):
        prob = jnp.exp(scores[t] - top_ref[1:2, :])
        grads[t * mp + mine] = (prob - jnp.where(is_target(t), F32(1.0), F32(0.0))).astype(BF16)
        for p in range(1, mp):
            share_grads(p, t).start()

    @pl.loop(FIRST, neg_groups)
    def _(k):
        share_negative(k)

    query_grad[...] = jnp.zeros_like(query_grad)

    @pl.loop(0, FIRST)
    def _(k):
        finish_negative(k)

    for t in range(neg_groups, groups):
        for p in range(1, mp):
            grads_from(p, t).wait_recv()
    for b in range(pos_blocks):
        value = candidate_grad(dp + b)
        upper = value.astype(BF16)
        high[b * PBS:(b + 1) * PBS, :] = upper
        low[b * PBS:(b + 1) * PBS, :] = (value - upper.astype(F32)).astype(BF16)

    @pl.loop(FIRST, neg_groups)
    def _(k):
        finish_negative(k)

    @pl.loop(neg_groups, groups)
    def _(t):
        add_query_grad(t)

    @pl.loop(0, table.shape[0] // 4)
    def _(c):
        ids = lax.broadcasted_iota(jnp.int32, (chunk, rows), 0) + c * chunk
        pick = jnp.where(ids == pos[...], 1.0, 0.0).astype(BF16)
        value = jnp.dot(pick, high[...], preferred_element_type=F32) + jnp.dot(
            pick, low[...], preferred_element_type=F32)
        base[pl.ds(c * 4, 4)] = value.reshape(4, PBS, width)

    @pl.loop(1, dp)
    def _(s):
        fetch(s).wait_send()
        give_back(s).wait()

    for p in range(1, mp):
        share_queries(p).wait_send()
        share_stats(p).wait_send()

        @pl.loop(0, groups)
        def _(t):
            relay(p, t).wait_send()
            share_grads(p, t).wait_send()


def assemble_kernel(
    dp, me_ref, neg, losses_in, query_grad_in, base, returned,
    losses, query_grad, out, stage, state, sems, loss_sem, query_sem,
):
    me = me_ref[0]
    block_count = base.shape[0]
    keep_losses = pltpu.make_async_copy(losses_in, losses, loss_sem)
    keep_losses.start()
    keep_query = pltpu.make_async_copy(query_grad_in, query_grad, query_sem)
    keep_query.start()

    @pl.loop(0, block_count)
    def _(k):
        state[k] = 0

    @pl.loop(0, dp)
    def _(s):
        k = neg[me ^ s, me]

        @pl.when(k >= 0)
        def _():
            state[k] = 1

    def plain(k):
        return pltpu.make_async_copy(base.at[k], out.at[k], sems.at[k])

    @pl.loop(0, block_count)
    def _(k):
        @pl.when(state[k] == 0)
        def _():
            plain(k).start()

    @pl.loop(0, dp)
    def _(s):
        k = neg[me ^ s, me]

        @pl.when(k >= 0)
        def _():
            now = state[k]

            @pl.when(now == 1)
            def _():
                state[k] = 2 + s
                stage[s] = base[k] + returned[s].astype(F32)

            @pl.when(now > 1)
            def _():
                stage[now - 2] += returned[s].astype(F32)

    @pl.loop(0, dp)
    def _(s):
        k = neg[me ^ s, me]

        @pl.when(k >= 0)
        def _():
            @pl.when(state[k] == 2 + s)
            def _():
                pltpu.make_async_copy(stage.at[s], out.at[k], sems.at[k]).start()

    keep_losses.wait()
    keep_query.wait()

    @pl.loop(0, block_count)
    def _(k):
        plain(k).wait()


def body(queries, passages, positives, negatives):
    dp = lax.axis_size("dp")
    mp = lax.axis_size("mp")
    rows, width = queries.shape
    factor = (width * mp) ** (-0.5)
    block_count = passages.shape[0] // PBS
    blocks = passages.reshape(block_count, PBS, width)
    total_blocks = dp + rows // PBS
    groups = total_blocks // mp
    vmem = pl.BlockSpec(memory_space=pltpu.VMEM)
    smem = pl.BlockSpec(memory_space=pltpu.SMEM)
    hbm = pl.BlockSpec(memory_space=pltpu.HBM)
    dma = pltpu.SemaphoreType.DMA
    made = (
        jax.ShapeDtypeStruct((1, rows), F32),
        jax.ShapeDtypeStruct((rows, width), F32),
        jax.ShapeDtypeStruct((block_count, PBS, width), F32),
        jax.ShapeDtypeStruct((dp, PBS, width), BF16),
    )
    scratch = [
        pltpu.VMEM((1, rows), jnp.int32),
        pltpu.VMEM((rows, width), BF16),
        pltpu.VMEM((rows, width), BF16),
        pltpu.VMEM((rows, width), BF16),
        pltpu.VMEM((block_count, PBS, width), BF16),
        pltpu.VMEM((dp, PBS, width), BF16),
        pltpu.VMEM((total_blocks, PBS, width), BF16),
        pltpu.VMEM((mp - 1, groups, PBS, width), BF16),
        pltpu.VMEM((mp - 1, rows, width), BF16),
        pltpu.VMEM((groups, PBS, rows), F32),
        pltpu.VMEM((total_blocks, PBS, rows), BF16),
        pltpu.VMEM((dp, PBS, width), BF16),
        pltpu.VMEM((mp, 8, rows), F32),
        pltpu.VMEM((8, rows), F32),
    ]
    held = sum(math.prod(a.shape) * jnp.dtype(a.dtype).itemsize for a in (*made, *scratch))
    losses, query_grad, base, returned = pl.pallas_call(
        functools.partial(exchange_kernel, dp, mp, factor),
        out_shape=made,
        in_specs=[hbm, hbm, hbm, hbm],
        out_specs=(vmem, vmem, vmem, vmem),
        scratch_shapes=[
            pltpu.SMEM((dp, dp), jnp.int32),
            *scratch,
            dma, dma, dma, dma,
            dma((dp,)), dma((dp,)), dma((mp - 1, groups)), dma((mp - 1, groups)),
            dma((mp - 1,)), dma((mp - 1,)), dma((mp - 1,)), dma((mp - 1,)),
            dma((mp - 1, groups)), dma((mp - 1, groups)), dma((dp,)), dma((dp,)),
        ],
        compiler_params=pltpu.CompilerParams(
            collective_id=0, has_side_effects=True, vmem_limit_bytes=held + 4 * 2**20),
    )(*(pltpu.with_memory_space_constraint(a, pltpu.HBM) for a in (negatives, positives.reshape(1, rows), queries, blocks)))
    losses, query_grad, passage_grad = pl.pallas_call(
        functools.partial(assemble_kernel, dp),
        out_shape=made[:3],
        in_specs=[smem, smem, vmem, vmem, vmem, vmem],
        out_specs=(hbm, hbm, hbm),
        scratch_shapes=[
            pltpu.VMEM((dp, PBS, width), F32),
            pltpu.SMEM((block_count,), jnp.int32),
            dma((block_count,)), dma, dma,
        ],
        compiler_params=pltpu.CompilerParams(vmem_limit_bytes=24 * 2**20),
    )(lax.axis_index("dp").reshape(1).astype(jnp.int32), negatives,
      losses, query_grad, base, returned)
    return losses.reshape(rows), query_grad, passage_grad.reshape(block_count * PBS, width)


def solution(mesh):
    in_specs = (P("dp", "mp"), P("dp", "mp"), P("dp"), P())
    out_specs = (P("dp"), P("dp", "mp"), P("dp", "mp"))
    return jax.shard_map(body, mesh=mesh, in_specs=in_specs, out_specs=out_specs, check_vma=False)
```
